32 devices in a mesh: req: 4 (over z), exp: 8 (over y, x, core).
Axes of the slice: x: 2, y: 2, z: 4, core: 2. Of those that a mesh axis runs over, the one named last changes fastest.
Arguments:
- hidden_in: bfloat16 [4096, 1024], P(('req', 'exp')), may hold values from -3 to 3
- queries: bfloat16 [4096, 1024], P(('req', 'exp')), may hold values from -9.5 to 9.5
- suffix_kv: bfloat16 [4096, 2048], P(('req', 'exp')), may hold values from -9.5 to 9.5
- request_ids: int32 [4096], P(('req', 'exp')), may hold values from 0 to 63, never falling along the last dimension, each value on 1 to 128 neighbouring positions
- group_of_request: int32 [64], replicated, may hold values from 0 to 3
- page_pool: bfloat16 [32, 128, 2048], P('exp'), may hold values from -9.5 to 9.5
- page_table: int32 [4, 8], replicated, may hold values from 0 to 31, as said below
- out_proj: bfloat16 [1024, 1024], replicated, may hold values from -0.1875 to 0.1875
- norm_gain: float32 [1024], replicated, may hold values from 0.1 to 1.9
- routes: int32 [4096, 2], P(('req', 'exp')), may hold values from 0 to 7, all different within a row; in each aligned block of 128 rows (0 to 127, 128 to 255, ...) at most 40 rows name the same one
- route_gates: float32 [4096, 2], P(('req', 'exp')), may hold values from 0.2 to 1
- w_gate: bfloat16 [8, 1024, 2816], P('exp'), may hold values from -0.1875 to 0.1875
- w_up: bfloat16 [8, 1024, 2816], P('exp'), may hold values from -0.1875 to 0.1875
- w_down: bfloat16 [8, 2816, 1024], P('exp'), may hold values from -0.109375 to 0.109375
Outputs:
- mixed: bfloat16 [4096, 1024], P(('req', 'exp'))
- layer_out: bfloat16 [4096, 1024], P(('req', 'exp'))
The draws below stay inside these ranges and needn't reach their ends.
Inputs may be any that keep to these rules, and one draw needn't show every extreme that they name: `request_ids`: ids never fall; each request has 1 to 128 consecutive tokens, one exactly 128. `page_table`: every page of the pool appears exactly once in the table. `routes`: each token names 2 different experts; in each aligned block of 128 tokens no expert is named more than 40 times, a bound that some block reaches.
All inputs are finite; a program needn't handle non-finite values.
Results may differ from the reference program's by a relative error of at most 0.015.
Values may be sent and summed in bfloat16 or wider, within the bound.
A program may use at most 192 MiB of HBM per device.

```python
import math
import jax
import jax.numpy as jnp
import numpy as np
from jax import lax

D = 1024
H = 16
HD = 64
FF = 2816
TOP = 2
PAGE = 128
PPG = 8
TOK_DEV = 128
POOL_DEV = 4
EXPERTS = 8
TOKENS = 4096
REQS = 64
POOL = 32
GROUPS = 4
CAP = 40
N_EXP = 8


def draw_queries(key, part):
    values = jnp.clip(jax.random.normal(jax.random.fold_in(key, 12), (TOKENS, D), jnp.float32), -6.0, 6.0)
    return values.astype(jnp.bfloat16)


def draw_suffix_kv(key, part):
    key_part = jnp.clip(jax.random.normal(jax.random.fold_in(key, 22), (TOKENS, D), jnp.float32), -6.0, 6.0)
    value_part = jnp.clip(jax.random.normal(jax.random.fold_in(key, 23), (TOKENS, D), jnp.float32), -6.0, 6.0)
    return jnp.concatenate([key_part, value_part], axis=1).astype(jnp.bfloat16)


def draw_page_pool(key, part):
    pool_rows = POOL * PAGE
    key_part = jnp.clip(jax.random.normal(jax.random.fold_in(key, 32), (pool_rows, D), jnp.float32), -6.0, 6.0)
    value_part = jnp.clip(jax.random.normal(jax.random.fold_in(key, 33), (pool_rows, D), jnp.float32), -6.0, 6.0)
    joined = jnp.concatenate([key_part, value_part], axis=1)
    return joined.reshape(POOL, PAGE, 2 * D).astype(jnp.bfloat16)


def draw_page_table(key, part):
    order = jax.random.permutation(jax.random.fold_in(key, 41), POOL)
    return order.astype(jnp.int32).reshape(GROUPS, PPG)


def place_ends(entries, own_key, low, largest):
    longest = entries.shape.index(max(entries.shape))
    spots = []
    for shift in (0, 1):
        where = [jax.random.randint(jax.random.fold_in(own_key, axis), (), 0, length) for axis, length in enumerate(entries.shape)]
        where[longest] = (where[longest] + shift) % entries.shape[longest]
        spots.append(tuple(where))
    return entries.at[spots[0]].set(low).at[spots[1]].set(largest)


def levels(rng, extent, cuts, least, top_value):
    loudness, own = 1.0, jax.random.fold_in(rng, 6)
    for dim, blocks in cuts:
        draws = jnp.exp(jax.random.uniform(jax.random.fold_in(own, dim), (blocks,), jnp.float32, least / len(cuts), top_value / len(cuts)))
        loudness = loudness * jnp.repeat(draws, extent[dim] // blocks).reshape([-1 if axis == dim else 1 for axis in range(len(extent))])
    return loudness


def rank_table(number_of, lean):
    weights = [(1 << 20) // math.isqrt(rank ** lean) + 1 for rank in range(1, number_of + 1)]
    scale = 1 + sum(weights) // (1 << 30)
    return np.cumsum(np.array([max(1, weight // scale) for weight in weights]))


def ranked(own_key, dims, amount, slope):
    table = rank_table(amount, slope)
    lot = jax.random.randint(jax.random.fold_in(own_key, 1), dims, 0, int(table[amount - 1]))
    grade = jnp.searchsorted(jnp.asarray(table, jnp.int32), lot, side="right")
    return jax.random.permutation(jax.random.fold_in(own_key, 2), amount)[grade].astype(jnp.int32)


def split_up(amount, total, most, lean):
    portions = [(1 << 20) // math.isqrt(standing ** lean) + 1 for standing in range(2, amount + 1)]
    spare, holding = total - most - (amount - 1), [1] * (amount - 1)
    while spare > 0:
        candidates = [i for i in range(amount - 1) if holding[i] < most]
        pool, left = sum([portions[i] for i in candidates]), spare
        for i in candidates:
            addition = min(most - holding[i], max(1, left * portions[i] // pool), spare)
            holding[i] = holding[i] + addition
            spare = spare - addition
    return np.array([most] + holding)


def ragged_sizes(key, count, total, most, lean):
    if count == 2:
        one = jax.random.randint(key, (), max(1, total - most), min(most, total - 1) + 1)
        return jnp.stack([one, total - one])
    lengths = jnp.asarray(split_up(count, total, most, lean), jnp.int32)
    twos = (count - 1) // 2
    giver, receiver = lengths[1:1 + 2 * twos:2], lengths[2:2 + 2 * twos:2]
    room = jnp.minimum(giver - 1, most - receiver)
    moved = jax.random.randint(jax.random.fold_in(key, 1), (twos,), 0, 1 << 20) % (room + 1)
    lengths = lengths.at[1:1 + 2 * twos:2].set(giver - moved).at[2:2 + 2 * twos:2].set(receiver + moved)
    return lengths[jax.random.permutation(jax.random.fold_in(key, 2), count)]


def shared_out(key, own, number, rows, count, top, limit, lean):
    order = jax.random.permutation(key, count)
    packed, usual = portions_of(count, rows * top, limit, lean, True), portions_of(count, rows * top, limit, lean, False)
    places = jnp.arange(count)

    def named(tallies, turn):
        used = int((tallies > 0).sum())
        fixed = max(1, used // 4)
        passed = fixed + (places - fixed + turn * (used - fixed)) % max(1, count - fixed)
        return jnp.zeros((count,), jnp.int32).at[order[jnp.where(places < fixed, places, passed)]].set(jnp.asarray(tallies, jnp.int32))

    tallies = jnp.where(number % 4 == 0, named(packed, number // 4), named(usual, number - number // 4 - 1))
    mixed = jax.random.permutation(jax.random.fold_in(own, 3), count)
    donor, receiver = mixed[0:count // 2 * 2:2], mixed[1:count // 2 * 2:2]
    margin = jnp.minimum(tallies[donor] - 1, limit - tallies[receiver]) // 2
    margin = jnp.where((donor == order[0]) | (receiver == order[0]) | (tallies[receiver] == 0), 0, jnp.maximum(margin, 0))
    passed = jax.random.randint(jax.random.fold_in(own, 4), (count // 2,), 0, 1 << 20) % (margin + 1)
    tallies = tallies.at[donor].add(-passed).at[receiver].add(passed)
    items = jnp.searchsorted(jnp.cumsum(tallies), jnp.arange(rows * top), side="right").astype(jnp.int32)
    grid = items.reshape(top, rows).T
    grid = grid[jax.random.permutation(jax.random.fold_in(own, 1), rows)]
    turn = jax.random.randint(jax.random.fold_in(own, 2), (rows, 1), 0, top)
    return jnp.take_along_axis(grid, (jnp.arange(top)[None, :] + turn) % top, axis=1)


def portions_of(amount, total, most, slope, full):
    portions = [(1 << 20) // math.isqrt(rank ** slope) + 1 for rank in range(1, amount + 1)]
    largest = most if full else min(most, max(-(-total // amount), total * portions[0] // sum(portions)))
    least = 1 if total - largest >= amount - 1 else 0
    counts, spare = [largest] + [least] * (amount - 1), total - largest - least * (amount - 1)
    while spare > 0:
        candidates = [i for i in range(1, amount) if counts[i] < largest] or [i for i in range(1, amount) if counts[i] < most]
        mass, remaining = sum([portions[i] for i in candidates]), spare
        for i in candidates:
            addition = min(most - counts[i], max(1, remaining * portions[i] // mass), spare)
            counts[i] = counts[i] + addition
            spare = spare - addition
    return np.array(counts)


def scatter_about(own_key, extent, scale, limit, pieces=(), kind=jnp.bfloat16):
    result = scale * jax.random.normal(own_key, extent, jnp.float32)
    if pieces:
        result = result * levels(own_key, extent, pieces, -0.22, 0.18)
    return jnp.clip(result, -limit, limit).astype(kind)


def setup_inputs(seed: int = 0) -> dict:
    arg_keys = jax.random.split(jax.random.key(seed), 15)
    hidden_in = scatter_about(arg_keys[0], (TOKENS, D), 0.5, 3.0, ((0, 32),))
    queries = draw_queries(jax.random.fold_in(arg_keys[14], 71), 0)
    suffix_kv = draw_suffix_kv(jax.random.fold_in(arg_keys[14], 71), 0)
    request_ids = jnp.searchsorted(jnp.cumsum(ragged_sizes(arg_keys[3], REQS, TOKENS, TOK_DEV, 2)), jnp.arange(TOKENS), side="right").astype(jnp.int32)
    group_of_request = place_ends(ranked(arg_keys[4], (REQS,), GROUPS, 2), jax.random.fold_in(arg_keys[4], 3), 0, GROUPS - 1).astype(jnp.int32)
    page_pool = draw_page_pool(jax.random.fold_in(arg_keys[14], 71), 0)
    page_table = draw_page_table(jax.random.fold_in(arg_keys[14], 71), 0)
    out_proj = scatter_about(arg_keys[7], (D, D), D ** -0.5, 0.1875)
    norm_gain = jnp.clip(1.0 + 0.18 * jax.random.normal(arg_keys[8], (D,), jnp.float32), 0.1, 1.9)
    routes_keys = jax.random.split(jax.random.fold_in(arg_keys[9], 1), TOKENS // TOK_DEV)
    routes_turns = jax.random.permutation(jax.random.fold_in(arg_keys[9], 3), TOKENS // TOK_DEV)
    routes = jax.vmap(lambda own, number: shared_out(jax.random.fold_in(arg_keys[9], 2), own, number, TOK_DEV, EXPERTS, TOP, CAP, 2))(routes_keys, routes_turns).reshape((TOKENS, TOP))
    route_gates = jnp.clip(0.2 + 0.8 * jax.random.uniform(arg_keys[10], (TOKENS, TOP), jnp.float32) ** levels(arg_keys[10], (TOKENS, TOP), ((0, 32),), -0.2, 0.2), 0.2, 1.0)
    w_gate = scatter_about(arg_keys[11], (EXPERTS, D, FF), D ** -0.5, 0.1875, ((0, 8),))
    w_up = scatter_about(arg_keys[12], (EXPERTS, D, FF), D ** -0.5, 0.1875, ((0, 8),))
    w_down = scatter_about(arg_keys[13], (EXPERTS, FF, D), FF ** -0.5, 0.109375, ((0, 8),))
    return {"hidden_in": hidden_in, "queries": queries, "suffix_kv": suffix_kv, "request_ids": request_ids, "group_of_request": group_of_request, "page_pool": page_pool, "page_table": page_table, "out_proj": out_proj, "norm_gain": norm_gain, "routes": routes, "route_gates": route_gates, "w_gate": w_gate, "w_up": w_up, "w_down": w_down}


MASKED = -1e+30

def partial_attend(query_heads, key_heads, value_heads, allowed):
    scaled = jnp.einsum('qhd,khd->qhk', query_heads.astype(jnp.float32), key_heads.astype(jnp.float32)) * (1.0 / math.sqrt(HD))
    allowed_heads = allowed[:, None, :]
    scaled = jnp.where(allowed_heads, scaled, MASKED)
    highest = lax.optimization_barrier(jnp.max(scaled, axis=-1))
    weights = jnp.where(allowed_heads, jnp.exp(scaled - highest[..., None]), 0.0)
    totals = lax.optimization_barrier(jnp.sum(weights, axis=-1))
    rounded = lax.optimization_barrier(weights.astype(jnp.bfloat16)).astype(jnp.float32)
    summed = jnp.einsum('qhk,khd->qhd', rounded, value_heads.astype(jnp.float32))
    return (highest, totals, summed)

def merge_partial(first_state, second_state):
    highest = jnp.maximum(first_state[0], second_state[0])
    first_scale = jnp.exp(first_state[0] - highest)
    second_scale = jnp.exp(second_state[0] - highest)
    totals = first_state[1] * first_scale + second_state[1] * second_scale
    summed = first_state[2] * first_scale[..., None] + second_state[2] * second_scale[..., None]
    return (highest, totals, summed)

def attend_all(queries, suffix_kv, request_ids, group_of_request, page_pool, page_table):
    token_group = jnp.take(group_of_request, request_ids)
    page_group = jnp.zeros((POOL,), jnp.int32).at[page_table.reshape(-1)].set(jnp.repeat(jnp.arange(GROUPS, dtype=jnp.int32), PPG))
    block_rows = math.gcd(TOKENS, 512)
    block_count = TOKENS // block_rows
    padded_kv = jnp.concatenate([jnp.zeros((TOK_DEV, 2 * D), suffix_kv.dtype), suffix_kv], 0)
    padded_ids = jnp.concatenate([jnp.full((TOK_DEV,), -1, jnp.int32), request_ids.astype(jnp.int32)], 0)
    pool_blocks = page_pool.reshape(N_EXP, POOL_DEV * PAGE, 2 * D)
    owner_blocks = jnp.repeat(page_group, PAGE).reshape(N_EXP, POOL_DEV * PAGE)

    def one_block(block_index):
        offset = (block_index * block_rows).astype(jnp.int32)
        query_heads = lax.dynamic_slice_in_dim(queries, offset, block_rows, 0).reshape(block_rows, H, HD)
        own_ids = lax.dynamic_slice_in_dim(request_ids, offset, block_rows, 0)
        own_groups = lax.dynamic_slice_in_dim(token_group, offset, block_rows, 0)
        window_kv = lax.dynamic_slice_in_dim(padded_kv, offset, block_rows + TOK_DEV, 0)
        window_ids = lax.dynamic_slice_in_dim(padded_ids, offset, block_rows + TOK_DEV, 0)
        query_pos = jnp.arange(block_rows, dtype=jnp.int32) + TOK_DEV
        key_pos = jnp.arange(block_rows + TOK_DEV, dtype=jnp.int32)
        allowed = (own_ids[:, None] == window_ids[None, :]) & (key_pos[None, :] <= query_pos[:, None])
        state = partial_attend(query_heads, window_kv[:, :D].reshape(-1, H, HD), window_kv[:, D:].reshape(-1, H, HD), allowed)

        def fold_pages(running, block_pair):
            pages, owners = block_pair
            allowed_pages = own_groups[:, None] == owners[None, :]
            highest, totals, summed = partial_attend(query_heads, pages[:, :D].reshape(-1, H, HD), pages[:, D:].reshape(-1, H, HD), allowed_pages)
            summed = lax.optimization_barrier(summed.astype(jnp.bfloat16)).astype(jnp.float32)
            return (merge_partial(running, (highest, totals, summed)), None)
        state, unused = lax.scan(fold_pages, state, (pool_blocks, owner_blocks))
        return (state[2] / state[1][..., None]).reshape(block_rows, D).astype(jnp.bfloat16)
    outputs = lax.map(one_block, jnp.arange(block_count, dtype=jnp.int32))
    return outputs.reshape(TOKENS, D)

def reference(hidden_in, queries, suffix_kv, request_ids, group_of_request, page_pool, page_table, out_proj, norm_gain, routes, route_gates, w_gate, w_up, w_down):
    attended = attend_all(queries, suffix_kv, request_ids, group_of_request, page_pool, page_table)
    mixed = (hidden_in.astype(jnp.float32) + jnp.dot(attended, out_proj, preferred_element_type=jnp.float32)).astype(jnp.bfloat16)
    wide = mixed.astype(jnp.float32)
    mean_square = lax.optimization_barrier(jnp.mean(wide * wide, axis=-1, keepdims=True))
    normed = (wide * lax.rsqrt(mean_square + 1e-06) * norm_gain).astype(jnp.bfloat16)
    blocks_count = TOKENS // TOK_DEV
    flat_routes = routes.reshape(blocks_count, TOK_DEV * TOP)
    hits = (flat_routes[..., None] == jnp.arange(EXPERTS, dtype=jnp.int32)).astype(jnp.int32)
    ranks = jnp.cumsum(hits, axis=1, dtype=jnp.int32) - 1
    slots = lax.optimization_barrier(jnp.sum(hits * ranks, axis=-1, dtype=jnp.int32)).reshape(TOKENS, TOP)
    block_of = (jnp.arange(TOKENS, dtype=jnp.int32) // TOK_DEV)[:, None]
    buffer_rows = (block_of * CAP + slots).astype(jnp.int32)
    buffers = jnp.zeros((EXPERTS, blocks_count * CAP, D), jnp.bfloat16)
    buffers = buffers.at[routes, buffer_rows].set(jnp.broadcast_to(normed[:, None, :], (TOKENS, TOP, D)))

    def expert_ffn(operands):
        rows_in, gate_w, up_w, down_w = operands
        gate_h = jnp.dot(rows_in, gate_w, preferred_element_type=jnp.float32)
        up_h = jnp.dot(rows_in, up_w, preferred_element_type=jnp.float32)
        activ = (jax.nn.gelu(gate_h, approximate=True) * up_h).astype(jnp.bfloat16)
        return jnp.dot(activ, down_w, preferred_element_type=jnp.float32).astype(jnp.bfloat16)
    results = lax.map(expert_ffn, (buffers, w_gate, w_up, w_down))
    picked = results[routes, buffer_rows]
    layer_out = (wide + lax.optimization_barrier(jnp.sum(route_gates[..., None] * picked.astype(jnp.float32), axis=1))).astype(jnp.bfloat16)
    return (mixed, layer_out)
```

```python
import functools

import jax
import jax.numpy as jnp
from jax import lax
from jax.experimental import pallas as pl
from jax.experimental.pallas import tpu as pltpu
from jax.sharding import PartitionSpec as P

HD = 64
LANES = 128
MASKED = -1e30
MESH = pl.DeviceIdType.MESH
F32 = jnp.float32
BF16 = jnp.bfloat16
FFN_SPLIT = 1


def xor(first, second, bits):
    total = 0
    for bit in range(bits):
        a = lax.rem(lax.div(first, jnp.int32(1 << bit)), jnp.int32(2))
        b = lax.rem(lax.div(jnp.int32(second), jnp.int32(1 << bit)), jnp.int32(2))
        total = total + (a + b - 2 * a * b) * (1 << bit)
    return total


def dot(a, b, contract=(1, 0)):
    return lax.dot_general(
        a, b, (((contract[0],), (contract[1],)), ((), ())), preferred_element_type=F32
    )


def iota(shape, dim):
    return lax.broadcasted_iota(jnp.int32, shape, dim)


def stack_heads(pair):
    wide = pair.astype(F32) * (1.0 / 8.0)
    low = iota(wide.shape, 1) < HD
    return jnp.concatenate(
        [jnp.where(low, wide, 0.0), jnp.where(low, 0.0, wide)], axis=0
    ).astype(BF16)


def soft_pair(scores, values):
    highest = jnp.max(scores, axis=1, keepdims=True)
    weights = jnp.exp(scores - highest).astype(BF16)
    both = dot(weights, jnp.concatenate([values, jnp.ones_like(values)], axis=1))
    totals = both[:, LANES:]
    return both[:, :LANES] / totals, highest + jnp.log(totals)


def kernel(
    n_req, n_exp, cap,
    hidden, queries, kv, ids, groups, pool, table, wo, gain, routes, gates, wg, wu, wd,
    mixed_out, layer_out,
    q_v, tg_v, pages_v, kaug_v, kv_v, kvp_v, ids_v, idp_v, hid_v, wo_v, wg_v, wu_v, wd_v,
    osend_v, orecv_v, lsend_v, lrecv_v, sufo_v, sufl_v, map_v, mix_v,
    disp_v, arr_v, act_v, fin_v, back_v,
    loc_sem, q_s, q_r, tg_s, tg_r, o_s, o_r, l_s, l_r, d_s, d_r, b_s, b_r, one_s, one_r,
):
    n_chip = n_exp // 2
    bits = (n_exp - 1).bit_length()
    rows, width = hid_v.shape
    pairs = width // LANES
    heads = width // HD
    per_dev = pool.shape[0]
    page = pool.shape[1]
    me_r = lax.axis_index("req")
    me = lax.axis_index("exp")
    total = n_req * n_exp
    flat = me_r * n_exp + me
    after = lax.rem(flat + 1, total)
    before = lax.rem(flat + total - 1, total)
    nxt = (lax.div(after, n_exp), lax.rem(after, n_exp))
    prv = (lax.div(before, n_exp), lax.rem(before, n_exp))
    peers = [None] + [xor(me, k, bits) for k in range(1, n_exp)]
    mate = peers[1]

    def local(src, dst, i):
        return pltpu.make_async_copy(src, dst, loc_sem.at[i])

    c_q = local(queries, q_v.at[0], 0)
    c_pages = local(pool, pages_v.at[pl.ds(0, per_dev)], 1)
    c_kv = local(kv, kv_v, 2)
    c_hid = local(hidden, hid_v, 3)
    c_wo = local(wo, wo_v, 4)
    c_wg = local(wg.at[0], wg_v, 5)
    c_wu = local(wu.at[0], wu_v, 6)
    c_wd = local(wd.at[0], wd_v, 7)
    c_q.start()
    c_pages.start()

    barrier = pltpu.get_barrier_semaphore()
    for peer in peers[1:]:
        pl.semaphore_signal(barrier, inc=1, device_id=(me_r, peer), device_id_type=MESH)
    pl.semaphore_signal(barrier, inc=1, device_id=nxt, device_id_type=MESH)
    pl.semaphore_signal(barrier, inc=1, device_id=prv, device_id_type=MESH)

    own_ids = ids[...]
    ids_v[...] = jnp.broadcast_to(own_ids, ids_v.shape)
    ids_tile = jnp.broadcast_to(own_ids, (8, rows))

    def add_group(r, acc):
        return jnp.where(ids_tile == r, groups[r], acc)

    tg_v[0] = lax.fori_loop(
        0, groups.shape[0], add_group, jnp.zeros((8, rows), jnp.int32), unroll=8
    )

    pl.semaphore_wait(barrier, n_exp + 1)

    def remote(src, dst, send, recv, device):
        return pltpu.make_async_remote_copy(
            src_ref=src, dst_ref=dst, send_sem=send, recv_sem=recv,
            device_id=device, device_id_type=MESH,
        )

    def chip_peer(k):
        return (me_r, xor(me, 2 * k, bits))

    def send_q(k):
        return remote(queries, q_v.at[k], q_s.at[k], q_r.at[k], chip_peer(k))

    def send_tg(k):
        return remote(tg_v.at[0], tg_v.at[k], tg_s.at[k], tg_r.at[k], chip_peer(k))

    def send_o(k):
        return remote(osend_v.at[k], orecv_v.at[k], o_s.at[k], o_r.at[k], chip_peer(k))

    def send_l(k):
        return remote(lsend_v.at[k], lrecv_v.at[k], l_s.at[k], l_r.at[k], chip_peer(k))

    s_pages = remote(
        pool, pages_v.at[pl.ds(per_dev, per_dev)], one_s.at[0], one_r.at[0], (me_r, mate)
    )
    s_kv = remote(kv, kvp_v, one_s.at[1], one_r.at[1], nxt)
    s_id = remote(ids_v, idp_v, one_s.at[2], one_r.at[2], nxt)

    s_pages.start()
    for k in range(1, n_chip):
        send_tg(k).start()
        send_q(k).start()
    s_id.start()
    s_kv.start()
    c_kv.start()
    c_hid.start()
    c_wo.start()
    c_wg.start()
    c_wu.start()
    c_wd.start()

    sub = iota((8, LANES), 0)
    n_slot = 2 * per_dev
    page_ids = jnp.where(sub < per_dev, me * per_dev + sub, mate * per_dev + sub - per_dev)
    owner = jnp.zeros((8, LANES), jnp.int32)
    for g in range(table.shape[0]):
        for i in range(table.shape[1]):
            owner = jnp.where(page_ids == table[g, i], g, owner)
    lane_page = iota((page, LANES), 1)
    for s in range(n_slot):
        kaug_v[s] = jnp.where(owner[s : s + 1, :] == lane_page, 1.0, 0.0).astype(BF16)

    lane = iota((rows, LANES), 1)
    gathered = jnp.where(
        lane == 0,
        routes[:, 0:1].astype(F32),
        jnp.where(
            lane == 1,
            routes[:, 1:2].astype(F32),
            jnp.where(lane == 2, gates[:, 0:1], gates[:, 1:2]),
        ),
    )
    turned = gathered.T
    r0, r1, g0, g1 = (turned[i : i + 1, :] for i in range(4))
    sub_e = iota((n_exp, rows), 0)
    experts = jnp.broadcast_to(me, (n_exp, rows))
    for k in range(1, n_exp):
        experts = jnp.where(sub_e == k, peers[k], experts)
    experts = experts.astype(F32)
    first = experts == r0
    second = experts == r1
    hit = jnp.where(first | second, 1.0, 0.0)
    gate = jnp.where(first, g0, g1)
    earlier = jnp.where(iota((rows, rows), 0) < iota((rows, rows), 1), 1.0, 0.0).astype(BF16)
    rank = dot(hit.astype(BF16), earlier)
    rank = jnp.where(hit > 0.0, rank, -1.0)
    slot = iota((cap, rows), 0).astype(F32)
    for k in range(n_exp):
        taken = jnp.where(rank[k : k + 1, :] == slot, 1.0, 0.0)
        weight = taken * gate[k : k + 1, :]
        high = weight.astype(BF16)
        at = pl.ds(k * cap, cap)
        map_v[0, at, :] = taken.astype(BF16)
        map_v[1, at, :] = high
        map_v[2, at, :] = (weight - high.astype(F32)).astype(BF16)

    c_q.wait()
    c_pages.wait()
    s_pages.wait_recv()

    def one_chip(k, carry):
        @pl.when(k > 0)
        def _():
            send_tg(k).wait_recv()
            send_q(k).wait_recv()

        group_col = jnp.broadcast_to(tg_v[k, 0:1, :].astype(F32), (LANES, rows)).T
        aug = jnp.where(group_col == lane.astype(F32), 0.0, MASKED)
        aug = jnp.concatenate([aug, aug], axis=0).astype(BF16)
        kaug = kaug_v[...].reshape(n_slot * page, LANES)

        def one_pair(p, logs):
            at = pl.ds(pl.multiple_of(p * LANES, LANES), LANES)
            vat = pl.ds(pl.multiple_of(width + p * LANES, LANES), LANES)
            left = jnp.concatenate([stack_heads(q_v[k, :, at]), aug], axis=1)
            keys = pages_v[:, :, at].reshape(n_slot * page, LANES)
            scores = dot(left, jnp.concatenate([keys, kaug], axis=1), (1, 1))
            values = pages_v[:, :, vat].reshape(n_slot * page, LANES)
            out, lse = soft_pair(scores, values)
            osend_v[k, :, at] = jnp.where(lane < HD, out[:rows], out[rows:]).astype(BF16)
            return jnp.where(
                lane == 2 * p, lse[:rows], jnp.where(lane == 2 * p + 1, lse[rows:], logs)
            )

        logs = lax.fori_loop(0, pairs, one_pair, jnp.zeros((rows, LANES), F32))
        lsend_v[k] = logs.T[:heads]

        @pl.when(k > 0)
        def _():
            send_o(k).start()
            send_l(k).start()

        return carry

    lax.fori_loop(0, n_chip, one_chip, 0)

    c_kv.wait()
    s_id.wait_recv()
    s_kv.wait_recv()
    id_col = jnp.broadcast_to(own_ids.astype(F32), (LANES, rows)).T
    past = jnp.where(flat > 0, idp_v[0:1, :].astype(F32), -1.0)
    bias_before = jnp.where(id_col == past, 0.0, MASKED)
    bias_own = jnp.where(
        (id_col == own_ids.astype(F32)) & (lane <= iota((rows, LANES), 0)), 0.0, MASKED
    )
    bias = jnp.concatenate([bias_before, bias_own], axis=1)

    def suffix_pair(p, logs):
        at = pl.ds(pl.multiple_of(p * LANES, LANES), LANES)
        vat = pl.ds(pl.multiple_of(width + p * LANES, LANES), LANES)
        keys = jnp.concatenate([kvp_v[:, at], kv_v[:, at]], axis=0)
        values = jnp.concatenate([kvp_v[:, vat], kv_v[:, vat]], axis=0)
        scores = dot(stack_heads(q_v[0, :, at]), keys, (1, 1))
        scores = scores + jnp.concatenate([bias, bias], axis=0)
        out, lse = soft_pair(scores, values)
        sufo_v[:, at] = jnp.where(lane < HD, out[:rows], out[rows:])
        return jnp.where(
            lane == 2 * p, lse[:rows], jnp.where(lane == 2 * p + 1, lse[rows:], logs)
        )

    suffix_logs = lax.fori_loop(0, pairs, suffix_pair, jnp.zeros((rows, LANES), F32))

    for k in range(1, n_chip):
        send_l(k).wait_recv()
        send_o(k).wait_recv()
    logs = [suffix_logs.T[:heads], lsend_v[0]] + [lrecv_v[k] for k in range(1, n_chip)]
    top = functools.reduce(jnp.maximum, logs)
    shares = [jnp.exp(entry - top) for entry in logs]
    below = functools.reduce(jnp.add, shares)
    spread = jnp.where(
        lax.rem(iota((2 * heads, width), 0), heads) == lax.div(iota((2 * heads, width), 1), HD),
        1.0,
        0.0,
    ).astype(BF16)
    attended = None
    for j, share in enumerate(shares):
        share = share / below
        high = share.astype(BF16)
        low = (share - high.astype(F32)).astype(BF16)
        scale = dot(jnp.concatenate([high, low], axis=0), spread, (0, 0))
        if j == 0:
            part = sufo_v[...]
        elif j == 1:
            part = osend_v[0].astype(F32)
        else:
            part = orecv_v[j - 1].astype(F32)
        attended = scale * part if attended is None else attended + scale * part
    c_wo.wait()
    c_hid.wait()
    mixed = (hid_v[...].astype(F32) + dot(attended.astype(BF16), wo_v[...])).astype(BF16)
    mixed_out[...] = mixed
    wide = mixed.astype(F32)
    mean_square = jnp.mean(wide * wide, axis=1, keepdims=True)
    mix_v[...] = (wide * lax.rsqrt(mean_square + 1e-6) * gain[...]).astype(BF16)

    def send_d(k):
        return remote(disp_v.at[k], arr_v.at[k], d_s.at[k], d_r.at[k], (me_r, peers[k]))

    def send_b(k):
        return remote(fin_v.at[k], back_v.at[k], b_s.at[k], b_r.at[k], (me_r, peers[k]))

    for k in reversed(range(n_exp)):
        out = dot(map_v[0, pl.ds(k * cap, cap), :], mix_v[...]).astype(BF16)
        if k > 0:
            disp_v[k] = out
            send_d(k).start()
        else:
            arr_v[0] = out

    tile = 256
    part = n_exp // FFN_SPLIT
    for half in range(FFN_SPLIT):
        slots = pl.ds(half * part, part)
        for k in range(half * part, (half + 1) * part):
            if k > 0:
                send_d(k).wait_recv()
        if half == 0:
            c_wg.wait()
            c_wu.wait()

        @pl.loop(0, wg_v.shape[1] // tile)
        def _(i):
            at = pl.ds(pl.multiple_of(i * tile, tile), tile)
            x = arr_v[slots].reshape(part * cap, width)
            gate_h = dot(x, wg_v[:, at])
            up_h = dot(x, wu_v[:, at])
            act_v[:, at] = (jax.nn.gelu(gate_h, approximate=True) * up_h).astype(BF16)

        if half == 0:
            c_wd.wait()

        @pl.loop(0, width // tile)
        def _(i):
            at = pl.ds(pl.multiple_of(i * tile, tile), tile)
            y = dot(act_v[...], wd_v[:, at]).astype(BF16)
            fin_v[slots, :, at] = y.reshape(part, cap, tile)

        for k in reversed(range(half * part, (half + 1) * part)):
            if k > 0:
                send_b(k).start()
            else:
                back_v[0] = fin_v[0]

    for k in range(1, n_exp):
        send_b(k).wait_recv()
    back = back_v[...].reshape(n_exp * cap, width)
    routed = dot(map_v[1], back, (0, 0)) + dot(map_v[2], back, (0, 0))
    layer_out[...] = (mixed_out[...].astype(F32) + routed).astype(BF16)

    s_pages.wait_send()
    s_kv.wait_send()
    s_id.wait_send()
    for k in range(1, n_chip):
        send_q(k).wait_send()
        send_tg(k).wait_send()
        send_o(k).wait_send()
        send_l(k).wait_send()
    for k in range(1, n_exp):
        send_d(k).wait_send()
        send_b(k).wait_send()


def body(
    n_req, n_exp,
    hidden_in, queries, suffix_kv, request_ids, group_of_request, page_pool, page_table,
    out_proj, norm_gain, routes, route_gates, w_gate, w_up, w_down,
):
    rows, width = queries.shape
    ff = w_gate.shape[2]
    per_dev, page = page_pool.shape[0], page_pool.shape[1]
    top_count = routes.shape[1]
    cap = (5 * rows * top_count + 4 * n_exp - 1) // (4 * n_exp)
    cap = (cap + 15) // 16 * 16
    n_chip = n_exp // 2
    heads = width // HD
    hbm = pl.BlockSpec(memory_space=pl.ANY)
    vmem = pl.BlockSpec(memory_space=pltpu.VMEM)
    smem = pl.BlockSpec(memory_space=pltpu.SMEM)
    dma = pltpu.SemaphoreType.DMA
    v = pltpu.VMEM
    out = jax.ShapeDtypeStruct((rows, width), BF16)
    part_rows = n_exp // FFN_SPLIT * cap
    return pl.pallas_call(
        functools.partial(kernel, n_req, n_exp, cap),
        out_shape=(out, out),
        in_specs=[
            hbm, hbm, hbm, vmem, smem, hbm, smem, hbm, vmem, vmem, vmem, hbm, hbm, hbm,
        ],
        out_specs=(vmem, vmem),
        scratch_shapes=[
            v((n_chip, rows, width), BF16),
            v((n_chip, 8, rows), jnp.int32),
            v((2 * per_dev, page, 2 * width), BF16),
            v((2 * per_dev, page, LANES), BF16),
            v((rows, 2 * width), BF16),
            v((rows, 2 * width), BF16),
            v((8, rows), jnp.int32),
            v((8, rows), jnp.int32),
            v((rows, width), BF16),
            v((width, width), BF16),
            v((width, ff), BF16),
            v((width, ff), BF16),
            v((ff, width), BF16),
            v((n_chip, rows, width), BF16),
            v((n_chip, rows, width), BF16),
            v((n_chip, heads, rows), F32),
            v((n_chip, heads, rows), F32),
            v((rows, width), F32),
            v((heads, rows), F32),
            v((3, n_exp * cap, rows), BF16),
            v((rows, width), BF16),
            v((n_exp, cap, width), BF16),
            v((n_exp, cap, width), BF16),
            v((part_rows, ff), BF16),
            v((n_exp, cap, width), BF16),
            v((n_exp, cap, width), BF16),
            dma((8,)),
            dma((n_chip,)), dma((n_chip,)),
            dma((n_chip,)), dma((n_chip,)),
            dma((n_chip,)), dma((n_chip,)),
            dma((n_chip,)), dma((n_chip,)),
            dma((n_exp,)), dma((n_exp,)),
            dma((n_exp,)), dma((n_exp,)),
            dma((3,)), dma((3,)),
        ],
        compiler_params=pltpu.CompilerParams(
            collective_id=0, has_side_effects=True, vmem_limit_bytes=58 * 1024 * 1024
        ),
        name="layer",
    )(
        hidden_in, queries, suffix_kv, request_ids.reshape(1, rows), group_of_request,
        page_pool, page_table, out_proj, norm_gain.reshape(1, width), routes, route_gates,
        w_gate, w_up, w_down,
    )


def solution(mesh):
    tokens = P(("req", "exp"), None)
    placed = (
        tokens, tokens, tokens, P(("req", "exp")), P(), P("exp", None, None), P(), P(), P(),
        tokens, tokens, P("exp", None, None), P("exp", None, None), P("exp", None, None),
    )
    return jax.shard_map(
        functools.partial(body, mesh.shape["req"], mesh.shape["exp"]),
        mesh=mesh,
        in_specs=placed,
        out_specs=(tokens, tokens),
        check_vma=False,
    )
```

```python
import functools

import jax
import jax.numpy as jnp
from jax import lax
from jax.experimental import pallas as pl
from jax.experimental.pallas import tpu as pltpu
from jax.sharding import PartitionSpec as P

HD = 64
LANES = 128
MASKED = -1e30
MESH = pl.DeviceIdType.MESH
F32 = jnp.float32
BF16 = jnp.bfloat16


def xor(first, second, bits):
    total = 0
    for bit in range(bits):
        a = lax.rem(lax.div(first, jnp.int32(1 << bit)), jnp.int32(2))
        b = lax.rem(lax.div(jnp.int32(second), jnp.int32(1 << bit)), jnp.int32(2))
        total = total + (a + b - 2 * a * b) * (1 << bit)
    return total


def dot(a, b, contract=(1, 0)):
    return lax.dot_general(
        a, b, (((contract[0],), (contract[1],)), ((), ())), preferred_element_type=F32
    )


def iota(shape, dim):
    return lax.broadcasted_iota(jnp.int32, shape, dim)


def stack_heads(pair):
    wide = pair.astype(F32) * (1.0 / 8.0)
    low = iota(wide.shape, 1) < HD
    return jnp.concatenate(
        [jnp.where(low, wide, 0.0), jnp.where(low, 0.0, wide)], axis=0
    ).astype(BF16)


def soft_pair(scores, values):
    highest = jnp.max(scores, axis=1, keepdims=True)
    weights = jnp.exp(scores - highest).astype(BF16)
    both = dot(weights, jnp.concatenate([values, jnp.ones_like(values)], axis=1))
    totals = both[:, LANES:]
    return both[:, :LANES] / totals, highest + jnp.log(totals)


def kernel(
    n_req, n_exp, cap,
    hidden, queries, kv, ids, groups, pool, table, wo, gain, routes, gates, wg, wu, wd,
    mixed_out, layer_out,
    q_v, tg_v, pages_v, kaug_v, kv_v, kvp_v, ids_v, idp_v, hid_v, wo_v, wg_v, wu_v, wd_v,
    osend_v, orecv_v, lsend_v, lrecv_v, sufo_v, map_v, comb_v, x_v, mix_v,
    disp_v, arr_v, act_v, fin_v, back_v,
    loc_sem, q_s, q_r, tg_s, tg_r, o_s, o_r, l_s, l_r, d_s, d_r, b_s, b_r, one_s, one_r,
):
    n_chip = n_exp // 2
    bits = (n_exp - 1).bit_length()
    rows, width = hid_v.shape
    pairs = width // LANES
    heads = width // HD
    per_dev = pool.shape[0]
    page = pool.shape[1]
    me_r = lax.axis_index("req")
    me = lax.axis_index("exp")
    total = n_req * n_exp
    flat = me_r * n_exp + me
    after = lax.rem(flat + 1, total)
    before = lax.rem(flat + total - 1, total)
    nxt = (lax.div(after, n_exp), lax.rem(after, n_exp))
    prv = (lax.div(before, n_exp), lax.rem(before, n_exp))
    peers = [None] + [xor(me, k, bits) for k in range(1, n_exp)]
    mate = peers[1]

    def local(src, dst, i):
        return pltpu.make_async_copy(src, dst, loc_sem.at[i])

    c_q = local(queries, q_v.at[0], 0)
    c_pages = local(pool, pages_v.at[pl.ds(0, per_dev)], 1)
    c_kv = local(kv, kv_v, 2)
    c_hid = local(hidden, hid_v, 3)
    c_wo = local(wo, wo_v, 4)
    c_wg = local(wg.at[0], wg_v, 5)
    c_wu = local(wu.at[0], wu_v, 6)
    c_wd = local(wd.at[0], wd_v, 7)
    c_q.start()
    c_pages.start()

    barrier = pltpu.get_barrier_semaphore()
    for peer in peers[1:]:
        pl.semaphore_signal(barrier, inc=1, device_id=(me_r, peer), device_id_type=MESH)
    pl.semaphore_signal(barrier, inc=1, device_id=nxt, device_id_type=MESH)
    pl.semaphore_signal(barrier, inc=1, device_id=prv, device_id_type=MESH)

    own_ids = ids[...]
    ids_v[...] = jnp.broadcast_to(own_ids, ids_v.shape)
    ids_tile = jnp.broadcast_to(own_ids, (8, rows))

    def add_group(r, acc):
        return jnp.where(ids_tile == r, groups[r], acc)

    tg_v[0] = lax.fori_loop(
        0, groups.shape[0], add_group, jnp.zeros((8, rows), jnp.int32), unroll=8
    )

    pl.semaphore_wait(barrier, n_exp + 1)

    def remote(src, dst, send, recv, device):
        return pltpu.make_async_remote_copy(
            src_ref=src, dst_ref=dst, send_sem=send, recv_sem=recv,
            device_id=device, device_id_type=MESH,
        )

    def chip_peer(k):
        return (me_r, xor(me, 2 * k, bits))

    def send_q(k):
        return remote(queries, q_v.at[k], q_s.at[k], q_r.at[k], chip_peer(k))

    def send_tg(k):
        return remote(tg_v.at[0], tg_v.at[k], tg_s.at[k], tg_r.at[k], chip_peer(k))

    def send_o(k):
        return remote(osend_v.at[k], orecv_v.at[k], o_s.at[k], o_r.at[k], chip_peer(k))

    def send_l(k):
        return remote(lsend_v.at[k], lrecv_v.at[k], l_s.at[k], l_r.at[k], chip_peer(k))

    s_pages = remote(
        pool, pages_v.at[pl.ds(per_dev, per_dev)], one_s.at[0], one_r.at[0], (me_r, mate)
    )
    s_kv = remote(kv, kvp_v, one_s.at[1], one_r.at[1], nxt)
    s_id = remote(ids_v, idp_v, one_s.at[2], one_r.at[2], nxt)

    s_pages.start()
    for k in range(1, n_chip):
        send_tg(k).start()
        send_q(k).start()
    s_id.start()
    s_kv.start()
    c_kv.start()
    c_hid.start()
    c_wo.start()
    c_wg.start()
    c_wu.start()
    c_wd.start()

    sub = iota((8, LANES), 0)
    n_slot = 2 * per_dev
    page_ids = jnp.where(sub < per_dev, me * per_dev + sub, mate * per_dev + sub - per_dev)
    owner = jnp.zeros((8, LANES), jnp.int32)
    for g in range(table.shape[0]):
        for i in range(table.shape[1]):
            owner = jnp.where(page_ids == table[g, i], g, owner)
    lane_page = iota((page, LANES), 1)
    for s in range(n_slot):
        kaug_v[s] = jnp.where(owner[s : s + 1, :] == lane_page, 1.0, 0.0).astype(BF16)

    lane = iota((rows, LANES), 1)
    r0, r1 = routes[0:1, :].astype(F32), routes[1:2, :].astype(F32)
    g0, g1 = gates[0:1, :], gates[1:2, :]
    sub_e = iota((n_exp, rows), 0)
    experts = jnp.broadcast_to(me, (n_exp, rows))
    for k in range(1, n_exp):
        experts = jnp.where(sub_e == k, peers[k], experts)
    experts = experts.astype(F32)
    first = experts == r0
    second = experts == r1
    hit = jnp.where(first | second, 1.0, 0.0)
    gate = jnp.where(first, g0, g1)
    earlier = jnp.where(iota((rows, rows), 0) < iota((rows, rows), 1), 1.0, 0.0).astype(BF16)
    rank = dot(hit.astype(BF16), earlier)
    rank = jnp.where(hit > 0.0, rank, -1.0)
    slot = iota((cap, rows), 0).astype(F32)
    taken = [jnp.where(rank[k : k + 1, :] == slot, 1.0, 0.0) for k in range(n_exp)]
    weight = [taken[k] * gate[k : k + 1, :] for k in range(n_exp)]
    map_v[...] = jnp.concatenate(taken, axis=0).astype(BF16)
    weight = jnp.concatenate(weight, axis=0).T
    high = weight.astype(BF16)
    comb_v[pl.ds(0, rows), :] = high
    comb_v[pl.ds(rows, rows), :] = (weight - high.astype(F32)).astype(BF16)

    c_q.wait()
    c_pages.wait()
    s_pages.wait_recv()

    def one_chip(k, carry):
        @pl.when(k > 0)
        def _():
            send_tg(k).wait_recv()
            send_q(k).wait_recv()

        group_col = jnp.broadcast_to(tg_v[k, 0:1, :].astype(F32), (LANES, rows)).T
        aug = jnp.where(group_col == lane.astype(F32), 0.0, MASKED)
        aug = jnp.concatenate([aug, aug], axis=0).astype(BF16)
        kaug = kaug_v[...].reshape(n_slot * page, LANES)

        def one_pair(p, logs):
            at = pl.ds(pl.multiple_of(p * LANES, LANES), LANES)
            vat = pl.ds(pl.multiple_of(width + p * LANES, LANES), LANES)
            left = jnp.concatenate([stack_heads(q_v[k, :, at]), aug], axis=1)
            keys = pages_v[:, :, at].reshape(n_slot * page, LANES)
            scores = dot(left, jnp.concatenate([keys, kaug], axis=1), (1, 1))
            values = pages_v[:, :, vat].reshape(n_slot * page, LANES)
            out, lse = soft_pair(scores, values)
            osend_v[k, :, at] = jnp.where(lane < HD, out[:rows], out[rows:]).astype(BF16)
            return jnp.where(
                lane == 2 * p, lse[:rows], jnp.where(lane == 2 * p + 1, lse[rows:], logs)
            )

        logs = lax.fori_loop(0, pairs, one_pair, jnp.zeros((rows, LANES), F32), unroll=8)
        lsend_v[k] = logs.T[:heads]

        @pl.when(k > 0)
        def _():
            send_o(k).start()
            send_l(k).start()

        return carry

    lax.fori_loop(0, n_chip, one_chip, 0)

    c_kv.wait()
    s_id.wait_recv()
    s_kv.wait_recv()
    id_col = jnp.broadcast_to(own_ids.astype(F32), (LANES, rows)).T
    past = jnp.where(flat > 0, idp_v[0:1, :].astype(F32), -1.0)
    bias_before = jnp.where(id_col == past, 0.0, MASKED)
    bias_own = jnp.where(
        (id_col == own_ids.astype(F32)) & (lane <= iota((rows, LANES), 0)), 0.0, MASKED
    )
    bias = jnp.concatenate([bias_before, bias_own], axis=1)

    def suffix_pair(p, logs):
        at = pl.ds(pl.multiple_of(p * LANES, LANES), LANES)
        vat = pl.ds(pl.multiple_of(width + p * LANES, LANES), LANES)
        keys = jnp.concatenate([kvp_v[:, at], kv_v[:, at]], axis=0)
        values = jnp.concatenate([kvp_v[:, vat], kv_v[:, vat]], axis=0)
        scores = dot(stack_heads(q_v[0, :, at]), keys, (1, 1))
        scores = scores + jnp.concatenate([bias, bias], axis=0)
        out, lse = soft_pair(scores, values)
        sufo_v[:, at] = jnp.where(lane < HD, out[:rows], out[rows:])
        return jnp.where(
            lane == 2 * p, lse[:rows], jnp.where(lane == 2 * p + 1, lse[rows:], logs)
        )

    suffix_logs = lax.fori_loop(0, pairs, suffix_pair, jnp.zeros((rows, LANES), F32), unroll=4)

    for k in range(1, n_chip):
        send_l(k).wait_recv()
        send_o(k).wait_recv()
    logs = [suffix_logs.T[:heads], lsend_v[0]] + [lrecv_v[k] for k in range(1, n_chip)]
    top = functools.reduce(jnp.maximum, logs)
    shares = [jnp.exp(entry - top) for entry in logs]
    below = functools.reduce(jnp.add, shares)
    spread = jnp.where(
        lax.rem(iota((2 * heads, width), 0), heads) == lax.div(iota((2 * heads, width), 1), HD),
        1.0,
        0.0,
    ).astype(BF16)
    shares = jnp.concatenate([share / below for share in shares], axis=1)
    high = shares.astype(BF16)
    low = (shares - high.astype(F32)).astype(BF16)
    scales = dot(jnp.concatenate([high, low], axis=0), spread, (0, 0))
    attended = scales[:rows] * sufo_v[...] + scales[rows : 2 * rows] * osend_v[0].astype(F32)
    for k in range(1, n_chip):
        at = (k + 1) * rows
        attended = attended + scales[at : at + rows] * orecv_v[k].astype(F32)
    c_wo.wait()
    c_hid.wait()
    mixed = (hid_v[...].astype(F32) + dot(attended.astype(BF16), wo_v[...])).astype(BF16)
    mixed_out[...] = mixed
    wide = mixed.astype(F32)
    mean_square = jnp.mean(wide * wide, axis=1, keepdims=True)
    mix_v[...] = (wide * lax.rsqrt(mean_square + 1e-6) * gain[...]).astype(BF16)

    def send_d(k):
        return remote(disp_v.at[k], arr_v.at[k], d_s.at[k], d_r.at[k], (me_r, peers[k]))

    def send_b(k):
        return remote(fin_v.at[k], back_v.at[k], b_s.at[k], b_r.at[k], (me_r, peers[k]))

    half = width // 2

    def fold(rows_in):
        grid = rows_in.reshape(n_exp, cap, rows_in.shape[1])
        cut = rows_in.shape[1] // 2
        return jnp.concatenate([grid[:, :, :cut], grid[:, :, cut:]], axis=1).astype(BF16)

    def unfold(ref):
        grid = ref[...].astype(F32)
        grid = jnp.concatenate([grid[:, :cap], grid[:, cap:]], axis=2)
        return grid.reshape(n_exp * cap, width).astype(BF16)

    disp_v[...] = fold(dot(map_v[...], mix_v[...]))
    for k in reversed(range(1, n_exp)):
        send_d(k).start()
    arr_v[0] = disp_v[0]
    for k in range(1, n_exp):
        send_d(k).wait_recv()
    x_v[...] = unfold(arr_v)
    c_wg.wait()
    c_wu.wait()
    tile = 256

    @pl.loop(0, wg_v.shape[1] // tile)
    def _(i):
        at = pl.ds(pl.multiple_of(i * tile, tile), tile)
        gate_h = dot(x_v[...], wg_v[:, at])
        up_h = dot(x_v[...], wu_v[:, at])
        act_v[:, at] = (jax.nn.gelu(gate_h, approximate=True) * up_h).astype(BF16)

    c_wd.wait()

    @pl.loop(0, half // tile)
    def _(i):
        at = pl.ds(pl.multiple_of(i * tile, tile), tile)
        far = pl.ds(pl.multiple_of(half + i * tile, tile), tile)
        near_y = dot(act_v[...], wd_v[:, at])
        far_y = dot(act_v[...], wd_v[:, far])
        fin_v[:, :, at] = fold(jnp.concatenate([near_y, far_y], axis=1))

    for k in reversed(range(1, n_exp)):
        send_b(k).start()
    back_v[0] = fin_v[0]

    for k in range(1, n_exp):
        send_b(k).wait_recv()
    both = dot(comb_v[...], unfold(back_v))
    routed = both[:rows] + both[rows:]
    layer_out[...] = (mixed_out[...].astype(F32) + routed).astype(BF16)

    s_pages.wait_send()
    s_kv.wait_send()
    s_id.wait_send()
    for k in range(1, n_chip):
        send_q(k).wait_send()
        send_tg(k).wait_send()
        send_o(k).wait_send()
        send_l(k).wait_send()
    for k in range(1, n_exp):
        send_d(k).wait_send()
        send_b(k).wait_send()


def hand_over(mixed, layer, mixed_out, layer_out, sem):
    first = pltpu.make_async_copy(mixed, mixed_out, sem.at[0])
    second = pltpu.make_async_copy(layer, layer_out, sem.at[1])
    first.start()
    second.start()
    first.wait()
    second.wait()


def body(
    n_req, n_exp,
    hidden_in, queries, suffix_kv, request_ids, group_of_request, page_pool, page_table,
    out_proj, norm_gain, routes, route_gates, w_gate, w_up, w_down,
):
    rows, width = queries.shape
    ff = w_gate.shape[2]
    per_dev, page = page_pool.shape[0], page_pool.shape[1]
    top_count = routes.shape[1]
    cap = (5 * rows * top_count + 4 * n_exp - 1) // (4 * n_exp)
    cap = (cap + 7) // 8 * 8
    n_chip = n_exp // 2
    heads = width // HD
    hbm = pl.BlockSpec(memory_space=pl.ANY)
    vmem = pl.BlockSpec(memory_space=pltpu.VMEM)
    smem = pl.BlockSpec(memory_space=pltpu.SMEM)
    dma = pltpu.SemaphoreType.DMA
    v = pltpu.VMEM
    out = jax.ShapeDtypeStruct((rows, width), BF16)
    results = pl.pallas_call(
        functools.partial(kernel, n_req, n_exp, cap),
        out_shape=(out, out),
        in_specs=[
            hbm, hbm, hbm, vmem, smem, hbm, smem, hbm, vmem, vmem, vmem, hbm, hbm, hbm,
        ],
        out_specs=(vmem, vmem),
        scratch_shapes=[
            v((n_chip, rows, width), BF16),
            v((n_chip, 8, rows), jnp.int32),
            v((2 * per_dev, page, 2 * width), BF16),
            v((2 * per_dev, page, LANES), BF16),
            v((rows, 2 * width), BF16),
            v((rows, 2 * width), BF16),
            v((8, rows), jnp.int32),
            v((8, rows), jnp.int32),
            v((rows, width), BF16),
            v((width, width), BF16),
            v((width, ff), BF16),
            v((width, ff), BF16),
            v((ff, width), BF16),
            v((n_chip, rows, width), BF16),
            v((n_chip, rows, width), BF16),
            v((n_chip, heads, rows), F32),
            v((n_chip, heads, rows), F32),
            v((rows, width), F32),
            v((n_exp * cap, rows), BF16),
            v((2 * rows, n_exp * cap), BF16),
            v((n_exp * cap, width), BF16),
            v((rows, width), BF16),
            v((n_exp, 2 * cap, width // 2), BF16),
            v((n_exp, 2 * cap, width // 2), BF16),
            v((n_exp * cap, ff), BF16),
            v((n_exp, 2 * cap, width // 2), BF16),
            v((n_exp, 2 * cap, width // 2), BF16),
            dma((8,)),
            dma((n_chip,)), dma((n_chip,)),
            dma((n_chip,)), dma((n_chip,)),
            dma((n_chip,)), dma((n_chip,)),
            dma((n_chip,)), dma((n_chip,)),
            dma((n_exp,)), dma((n_exp,)),
            dma((n_exp,)), dma((n_exp,)),
            dma((3,)), dma((3,)),
        ],
        compiler_params=pltpu.CompilerParams(
            collective_id=0, has_side_effects=True, vmem_limit_bytes=58 * 1024 * 1024
        ),
        name="layer",
    )(
        hidden_in, queries, suffix_kv, request_ids.reshape(1, rows), group_of_request,
        page_pool, page_table, out_proj, norm_gain.reshape(1, width), routes.T, route_gates.T,
        w_gate, w_up, w_down,
    )
    return results


def solution(mesh):
    tokens = P(("req", "exp"), None)
    placed = (
        tokens, tokens, tokens, P(("req", "exp")), P(), P("exp", None, None), P(), P(), P(),
        tokens, tokens, P("exp", None, None), P("exp", None, None), P("exp", None, None),
    )
    return jax.shard_map(
        functools.partial(body, mesh.shape["req"], mesh.shape["exp"]),
        mesh=mesh,
        in_specs=placed,
        out_specs=(tokens, tokens),
        check_vma=False,
    )
```
